32 devices in a mesh: grp: 2 (over y), rows: 8 (over z, x), mod: 2 (over core).
Axes of the slice: x: 2, y: 2, z: 4, core: 2. Of those that a mesh axis runs over, the one named last changes fastest.
Arguments:
- queries: bfloat16 [16, 8, 2304], P(('grp', 'rows'), 'mod'), parts along dimension 0, may hold values from -6 to 6
- train_grads: bfloat16 [2048, 8, 2304], P(('grp', 'rows'), 'mod'), parts along dimension 0, may hold values from -6 to 6
- factors: float32 [8, 2, 48, 48], P('mod'), may hold values from -4 to 4, as said below
Outputs:
- scores: float32 [16, 1024], P(('grp', 'mod'), 'rows'), parts along dimension 0
The draws below stay inside these ranges and needn't reach their ends.
There are 2 independent parts, one for each index of `grp`. The reference program is written for one: setup_inputs(seed, part) draws one part's arguments, and reference() takes and returns one part's arrays. A program takes and returns all parts, laid end to end along the dimension named above; an argument that names none is the same for every part. Nothing has to cross between parts.
Inputs may be any that keep to these rules, and one draw needn't show every extreme that they name: `factors`: each factor is a 48 x 48 matrix with a positive diagonal and full rank.
All inputs are finite; a program needn't handle non-finite values.
Results may differ from the reference program's by a relative error of at most 0.0029.
Values may be sent and summed in bfloat16 or wider, within the bound.
A program may use at most 64 MiB of HBM per device.

```python
import jax
import jax.numpy as jnp
from jax import lax

MODULES = 8
PROJ = 48
T_DEV = 128
COORDS = 2304
NQ = 8
NTRAIN = 1024
N_ROWS = 8


def draw_factors(key, part):
    key_diag, key_off = jax.random.split(jax.random.fold_in(key, 17))
    shape = (MODULES, 2, PROJ, PROJ)
    diag_vals = jnp.exp(jax.random.uniform(key_diag, (MODULES, 2, PROJ), jnp.float32, jnp.log(0.5), jnp.log(2.0)))
    off_vals = jnp.clip(jax.random.normal(key_off, shape, jnp.float32), -4.0, 4.0) * (0.5 / jnp.sqrt(jnp.float32(PROJ)))
    eye_mask = jnp.eye(PROJ, dtype=jnp.float32)
    return off_vals * (1.0 - eye_mask) + diag_vals[..., None] * eye_mask


def levels(stream_key, dims, pieces, least, largest):
    level, own = 1.0, jax.random.fold_in(stream_key, 6)
    for dim, blocks in pieces:
        heights = jnp.exp(jax.random.uniform(jax.random.fold_in(own, dim), (blocks,), jnp.float32, least / len(pieces), largest / len(pieces)))
        level = level * jnp.repeat(heights, dims[dim] // blocks).reshape([-1 if axis == dim else 1 for axis in range(len(dims))])
    return level


def scatter_about(rng, extent, width, limit, pieces=(), kind=jnp.bfloat16):
    entries = width * jax.random.normal(rng, extent, jnp.float32)
    if pieces:
        entries = entries * levels(rng, extent, pieces, -0.22, 0.18)
    return jnp.clip(entries, -limit, limit).astype(kind)


def setup_inputs(seed: int = 0, part: int = 0) -> dict:
    splits = jax.random.split(jax.random.key(seed), 4)
    own_keys = jax.random.split(jax.random.fold_in(splits[3], part), 4)
    queries = scatter_about(own_keys[0], (NQ, MODULES, COORDS), 1.0, 6.0, ((0, 8), (1, 2)))
    train_grads = scatter_about(own_keys[1], (NTRAIN, MODULES, COORDS), 1.0, 6.0, ((0, 8), (1, 2)))
    factors = draw_factors(jax.random.fold_in(splits[3], 71), part)
    return {"queries": queries, "train_grads": train_grads, "factors": factors}


def precondition(queries, factors):
    count = queries.shape[0]
    grads = queries.astype(jnp.float32).reshape(count, MODULES, PROJ, PROJ)
    left_side = jnp.einsum('mab,qmbc->qmac', factors[:, 0], grads, precision=lax.Precision.HIGHEST)
    both_sides = jnp.einsum('qmac,mcd->qmad', left_side, factors[:, 1], precision=lax.Precision.HIGHEST)
    both_sides = both_sides / jnp.sqrt(jnp.float32(MODULES * COORDS))
    return both_sides.astype(jnp.bfloat16).reshape(count, MODULES * COORDS)

def reference(queries, train_grads, factors):
    scaled = precondition(queries, factors)
    blocks = train_grads.reshape(N_ROWS, T_DEV, MODULES * COORDS)

    def score_block(block):
        return lax.dot_general(scaled, block, (((1,), (1,)), ((), ())), preferred_element_type=jnp.float32)
    parts = lax.map(score_block, blocks)
    return jnp.transpose(parts, (1, 0, 2)).reshape(scaled.shape[0], N_ROWS * T_DEV)
```

```python
import functools
import math

import jax
import jax.numpy as jnp
from jax import lax
from jax.experimental import pallas as pl
from jax.experimental.pallas import tpu as pltpu
from jax.sharding import PartitionSpec as P

HIGHEST = lax.Precision.HIGHEST
LANES = 128
GROUP = 8


def iota(shape, dim):
    return lax.broadcasted_iota(jnp.int32, shape, dim)


def zero_one(mask):
    return jnp.where(mask, 1.0, 0.0).astype(jnp.bfloat16)


def dot(a, b, contract, precision=None):
    return lax.dot_general(
        a, b, ((contract[:1], contract[1:]), ((), ())), precision=precision, preferred_element_type=jnp.float32
    )


def precondition(query, factors, scale, modules, side):
    chunks = side // GROUP
    width = GROUP * side
    rows = modules * side
    flat = jnp.concatenate([query[:, c * width : (c + 1) * width] for c in range(chunks)], axis=0)
    spread = zero_one(
        iota((rows, chunks * modules), 1)
        == (iota((rows, chunks * modules), 0) % side) // GROUP * modules + iota((rows, chunks * modules), 0) // side
    )
    keep = iota((rows, width), 0) % GROUP == iota((rows, width), 1) // side
    fold = zero_one(iota((width, side), 0) % side == iota((width, side), 1))
    matrices = dot(spread, flat.astype(jnp.bfloat16), (1, 0))
    matrices = jnp.where(keep, matrices, 0.0).astype(jnp.bfloat16)
    matrices = dot(matrices, fold, (1, 0))
    outs = []
    for m in range(modules):
        left = dot(factors[m, 0], matrices[m * side : (m + 1) * side], (1, 0), HIGHEST)
        outs.append(dot(left, factors[m, 1], (1, 0), HIGHEST))
    both = (jnp.concatenate(outs, axis=0) / scale).astype(jnp.bfloat16)
    wide = dot(both, fold, (1, 1))
    wide = jnp.where(keep, wide, 0.0).astype(jnp.bfloat16)
    return dot(spread, wide, (0, 0))


def kernel(
    rows_n, grp_scale, q_hbm, t_hbm, f_hbm, out_ref,
    q_v, f_v, t_v, own, held, part, other,
    in_sem, t_sem, send_sem, recv_sem, ex_sem,
):
    modules, coords = q_hbm.shape[1:]
    side = f_hbm.shape[-1]
    tiles = coords // LANES
    train = t_hbm.shape[0]
    me = lax.axis_index("rows")
    core = lax.axis_index("mod")

    q_copy = pltpu.make_async_copy(q_hbm, q_v, in_sem.at[0])
    f_copy = pltpu.make_async_copy(f_hbm, f_v, in_sem.at[1])
    q_copy.start()
    f_copy.start()

    barrier = pltpu.get_barrier_semaphore()
    for step in range(1, rows_n):
        pl.semaphore_signal(barrier, inc=1, device_id={"rows": lax.rem(me + step, rows_n)})
    pl.semaphore_signal(barrier, inc=1, device_id={"mod": 1 - core})

    t_copies = [
        pltpu.make_async_copy(t_hbm.at[:, :, pl.ds(j * LANES, LANES)], t_v.at[j], t_sem.at[j]) for j in range(tiles)
    ]
    for copy in t_copies:
        copy.start()

    q_copy.wait()
    f_copy.wait()
    scaled = precondition(q_v[0].astype(jnp.float32), f_v, grp_scale, modules, side)
    per = GROUP * side // LANES
    for j in range(tiles):
        c, t = divmod(j, per)
        piece = scaled[c * modules : (c + 1) * modules, t * LANES : (t + 1) * LANES].astype(jnp.bfloat16)
        own[j] = piece

    pl.semaphore_wait(barrier, rows_n)

    def push(step):
        return pltpu.make_async_remote_copy(
            src_ref=own,
            dst_ref=held.at[me],
            send_sem=send_sem.at[step],
            recv_sem=recv_sem.at[step],
            device_id={"rows": lax.rem(me + step, rows_n)},
        )

    def arrival(step):
        source = lax.rem(me + rows_n - step, rows_n)
        return pltpu.make_async_remote_copy(
            src_ref=own,
            dst_ref=held.at[source],
            send_sem=send_sem.at[step],
            recv_sem=recv_sem.at[step],
            device_id={"rows": lax.rem(me + step, rows_n)},
        )

    for step in range(1, rows_n):
        push(step).start()
    held[me] = own[...]
    for copy in t_copies:
        copy.wait()
    for step in range(1, rows_n):
        arrival(step).wait_recv()

    total = jnp.zeros((train * modules, rows_n * modules), jnp.float32)
    for j in range(tiles):
        a = t_v[j].reshape(train * modules, LANES)
        b = held[:, j].reshape(rows_n * modules, LANES)
        total += dot(a, b, (1, 1))
    same = iota(total.shape, 0) % modules == iota(total.shape, 1) % modules
    total = jnp.where(same, total, 0.0)
    pick_n = jnp.where(iota((train * modules, train), 0) // modules == iota((train * modules, train), 1), 1.0, 0.0)
    pick_q = jnp.where(iota((rows_n, rows_n * modules), 1) // modules == iota((rows_n, rows_n * modules), 0), 1.0, 0.0)
    by_n = dot(pick_n, total, (0, 0), HIGHEST)
    scores = dot(pick_q, by_n, (1, 1), HIGHEST)
    half = rows_n // 2
    part[0] = scores[:half]
    part[1] = scores[half:]
    swap = pltpu.make_async_remote_copy(
        src_ref=part.at[1 - core],
        dst_ref=other,
        send_sem=ex_sem.at[0],
        recv_sem=ex_sem.at[1],
        device_id={"mod": 1 - core},
    )
    swap.start()
    swap.wait_recv()
    out_ref[...] = part[core] + other[...]
    swap.wait_send()
    for step in range(1, rows_n):
        push(step).wait_send()


def shards(rows_n, cores, queries, train_grads, factors):
    _, modules, coords = queries.shape
    train = train_grads.shape[0]
    side = factors.shape[-1]
    tiles = coords // LANES
    scale = math.sqrt(cores * modules * coords)
    half = rows_n // 2
    return pl.pallas_call(
        functools.partial(kernel, rows_n, scale),
        out_shape=jax.ShapeDtypeStruct((half, train), jnp.float32),
        in_specs=[pl.BlockSpec(memory_space=pl.ANY)] * 3,
        out_specs=pl.BlockSpec(memory_space=pltpu.VMEM),
        scratch_shapes=[
            pltpu.VMEM(queries.shape, jnp.bfloat16),
            pltpu.VMEM(factors.shape, jnp.float32),
            pltpu.VMEM((tiles, train, modules, LANES), jnp.bfloat16),
            pltpu.VMEM((tiles, modules, LANES), jnp.bfloat16),
            pltpu.VMEM((rows_n, tiles, modules, LANES), jnp.bfloat16),
            pltpu.VMEM((2, half, train), jnp.float32),
            pltpu.VMEM((half, train), jnp.float32),
            pltpu.SemaphoreType.DMA((2,)),
            pltpu.SemaphoreType.DMA((tiles,)),
            pltpu.SemaphoreType.DMA((rows_n,)),
            pltpu.SemaphoreType.DMA((rows_n,)),
            pltpu.SemaphoreType.DMA((2,)),
        ],
        compiler_params=pltpu.CompilerParams(
            collective_id=0, has_side_effects=True, vmem_limit_bytes=32 * 1024 * 1024
        ),
    )(queries, train_grads, factors)


def solution(mesh):
    in_specs = (
        P(("grp", "rows"), "mod", None),
        P(("grp", "rows"), "mod", None),
        P("mod", None, None, None),
    )
    out_specs = P(("grp", "mod"), "rows")
    body = functools.partial(shards, mesh.shape["rows"], mesh.shape["mod"])
    return jax.shard_map(body, mesh=mesh, in_specs=in_specs, out_specs=out_specs, check_vma=False)
```

```python
import functools
import math

import jax
import jax.numpy as jnp
from jax import lax
from jax.experimental import pallas as pl
from jax.experimental.pallas import tpu as pltpu
from jax.sharding import PartitionSpec as P

HIGHEST = lax.Precision.HIGHEST
LANES = 128
GROUP = 8


def iota(shape, dim):
    return lax.broadcasted_iota(jnp.int32, shape, dim)


def zero_one(mask):
    return jnp.where(mask, 1.0, 0.0).astype(jnp.bfloat16)


def dot(a, b, contract, precision=None):
    return lax.dot_general(
        a, b, ((contract[:1], contract[1:]), ((), ())), precision=precision, preferred_element_type=jnp.float32
    )


def split(x):
    high = x.astype(jnp.bfloat16)
    return high, (x - high.astype(jnp.float32)).astype(jnp.bfloat16)


def precondition(query, factors, scale, modules, side):
    chunks = side // GROUP
    width = GROUP * side
    rows = modules * side
    keep = iota((rows, width), 0) % GROUP == iota((rows, width), 1) // side
    fold = zero_one(iota((width, rows), 0) % side == iota((width, rows), 1) % side)
    tile = zero_one(iota((side, width), 0) == iota((side, width), 1) % side)
    gather = zero_one(
        iota((chunks * modules, rows), 0)
        == (iota((chunks * modules, rows), 1) % side) // GROUP * modules + iota((chunks * modules, rows), 1) // side
    )
    block = iota((rows, rows), 0) // side == iota((rows, rows), 1) // side

    spread = [
        jnp.broadcast_to(query[m : m + 1, c * width : (c + 1) * width], (GROUP, width))
        for m in range(modules)
        for c in range(chunks)
    ]
    spread = jnp.where(keep, jnp.concatenate(spread, axis=0), 0.0).astype(jnp.bfloat16)
    matrices = dot(spread, fold, (1, 0)).astype(jnp.bfloat16)

    lefts = jnp.concatenate([factors[m, 0] for m in range(modules)], axis=0)
    lefts = jnp.where(block, jnp.concatenate([lefts] * modules, axis=1), 0.0)
    left_high, left_low = split(lefts)
    left = dot(left_high, matrices, (1, 0)) + dot(left_low, matrices, (1, 0))
    left = jnp.where(block, left, 0.0)
    high, low = split(left)

    rights = jnp.concatenate([factors[m, 1] for m in range(modules)], axis=0)
    right_high, right_low = split(rights)
    right_high = dot(right_high, tile, (1, 0)).astype(jnp.bfloat16)
    right_low = dot(right_low, tile, (1, 0)).astype(jnp.bfloat16)
    both = dot(high, right_high, (1, 0)) + (dot(low, right_high, (1, 0)) + dot(high, right_low, (1, 0)))
    both = jnp.where(keep, both * (1.0 / scale), 0.0).astype(jnp.bfloat16)
    return dot(gather, both, (1, 0))


def kernel(
    rows_n, grp_scale, q_hbm, t_hbm, f_hbm, out_ref,
    q_v, f_v, t_v, own, held, part, other, pairs,
    in_sem, t_sem, send_sem, recv_sem, ex_sem,
):
    modules, coords = q_hbm.shape[1:]
    side = f_hbm.shape[-1]
    tiles = coords // LANES
    train = t_hbm.shape[0]
    me = lax.axis_index("rows")
    core = lax.axis_index("mod")

    q_copy = pltpu.make_async_copy(q_hbm, q_v, in_sem.at[0])
    f_copy = pltpu.make_async_copy(f_hbm, f_v, in_sem.at[1])
    q_copy.start()
    f_copy.start()

    barrier = pltpu.get_barrier_semaphore()
    for step in range(1, rows_n):
        pl.semaphore_signal(barrier, inc=1, device_id={"rows": lax.rem(me + step, rows_n)})
    pl.semaphore_signal(barrier, inc=1, device_id={"mod": 1 - core})

    t_copies = [
        pltpu.make_async_copy(t_hbm.at[:, :, pl.ds(j * LANES, LANES)], t_v.at[j], t_sem.at[j]) for j in range(tiles)
    ]
    for copy in t_copies:
        copy.start()

    q_copy.wait()
    f_copy.wait()
    scaled = precondition(q_v[0].astype(jnp.float32), f_v, grp_scale, modules, side)
    per = GROUP * side // LANES
    for j in range(tiles):
        c, t = divmod(j, per)
        piece = scaled[c * modules : (c + 1) * modules, t * LANES : (t + 1) * LANES].astype(jnp.bfloat16)
        own[j] = piece

    pl.semaphore_wait(barrier, rows_n)

    def push(step):
        return pltpu.make_async_remote_copy(
            src_ref=own,
            dst_ref=held.at[me],
            send_sem=send_sem.at[step],
            recv_sem=recv_sem.at[step],
            device_id={"rows": lax.rem(me + step, rows_n)},
        )

    def arrival(step):
        source = lax.rem(me + rows_n - step, rows_n)
        return pltpu.make_async_remote_copy(
            src_ref=own,
            dst_ref=held.at[source],
            send_sem=send_sem.at[step],
            recv_sem=recv_sem.at[step],
            device_id={"rows": lax.rem(me + step, rows_n)},
        )

    for step in range(1, rows_n):
        push(step).start()
    held[me] = own[...]
    for copy in t_copies:
        copy.wait()
    for step in range(1, rows_n):
        arrival(step).wait_recv()

    total = jnp.zeros((rows_n * modules, train * modules), jnp.float32)
    a = jnp.concatenate([t_v[j].reshape(train * modules, LANES) for j in range(tiles)], axis=1)
    b = jnp.concatenate([held[:, j].reshape(rows_n * modules, LANES) for j in range(tiles)], axis=1)
    total = dot(b, a, (1, 1))
    for k in range(train * modules // LANES):
        pairs[k] = total[:, k * LANES : (k + 1) * LANES]
    shape = (rows_n, train * modules)
    which = iota(shape, 1) % modules
    kept = jnp.zeros(shape, jnp.float32)
    for m in range(modules):
        some = [pairs[k, pl.ds(m, rows_n, stride=modules), :] for k in range(train * modules // LANES)]
        kept = jnp.where(which == m, jnp.concatenate(some, axis=1), kept)
    pick = zero_one(iota((train * modules, train), 0) // modules == iota((train * modules, train), 1))
    high, low = split(kept)
    low2 = (kept - high.astype(jnp.float32) - low.astype(jnp.float32)).astype(jnp.bfloat16)
    summed = dot(jnp.concatenate([high, low, low2], axis=0), pick, (1, 0))
    scores = summed[:rows_n] + (summed[rows_n : 2 * rows_n] + summed[2 * rows_n :])
    half = rows_n // 2
    part[0] = scores[:half]
    part[1] = scores[half:]
    swap = pltpu.make_async_remote_copy(
        src_ref=part.at[1 - core],
        dst_ref=other,
        send_sem=ex_sem.at[0],
        recv_sem=ex_sem.at[1],
        device_id={"mod": 1 - core},
    )
    swap.start()
    swap.wait_recv()
    out_ref[...] = part[core] + other[...]
    swap.wait_send()
    for step in range(1, rows_n):
        push(step).wait_send()


def shards(rows_n, cores, queries, train_grads, factors):
    _, modules, coords = queries.shape
    train = train_grads.shape[0]
    side = factors.shape[-1]
    tiles = coords // LANES
    scale = math.sqrt(cores * modules * coords)
    half = rows_n // 2
    return pl.pallas_call(
        functools.partial(kernel, rows_n, scale),
        out_shape=pltpu.VMEM((half, train), jnp.float32),
        in_specs=[pl.BlockSpec(memory_space=pltpu.HBM)] * 3,
        out_specs=pl.BlockSpec(memory_space=pltpu.VMEM),
        scratch_shapes=[
            pltpu.VMEM(queries.shape, jnp.bfloat16),
            pltpu.VMEM(factors.shape, jnp.float32),
            pltpu.VMEM((tiles, train, modules, LANES), jnp.bfloat16),
            pltpu.VMEM((tiles, modules, LANES), jnp.bfloat16),
            pltpu.VMEM((rows_n, tiles, modules, LANES), jnp.bfloat16),
            pltpu.VMEM((2, half, train), jnp.float32),
            pltpu.VMEM((half, train), jnp.float32),
            pltpu.VMEM((train * modules // LANES, rows_n * modules, LANES), jnp.float32),
            pltpu.SemaphoreType.DMA((2,)),
            pltpu.SemaphoreType.DMA((tiles,)),
            pltpu.SemaphoreType.DMA((rows_n,)),
            pltpu.SemaphoreType.DMA((rows_n,)),
            pltpu.SemaphoreType.DMA((2,)),
        ],
        compiler_params=pltpu.CompilerParams(
            collective_id=0, has_side_effects=True, vmem_limit_bytes=60 * 1024 * 1024
        ),
    )(queries, train_grads, factors)


def solution(mesh):
    in_specs = (
        P(("grp", "rows"), "mod", None),
        P(("grp", "rows"), "mod", None),
        P("mod", None, None, None),
    )
    out_specs = P(("grp", "mod"), "rows")
    body = functools.partial(shards, mesh.shape["rows"], mesh.shape["mod"])
    return jax.shard_map(body, mesh=mesh, in_specs=in_specs, out_specs=out_specs, check_vma=False)
```

```python
import functools
import math

import jax
import jax.numpy as jnp
from jax import lax
from jax.experimental import pallas as pl
from jax.experimental.pallas import tpu as pltpu
from jax.sharding import PartitionSpec as P

HIGHEST = lax.Precision.HIGHEST
LANES = 128
GROUP = 8


def iota(shape, dim):
    return lax.broadcasted_iota(jnp.int32, shape, dim)


def zero_one(mask):
    return jnp.where(mask, 1.0, 0.0).astype(jnp.bfloat16)


def dot(a, b, contract, precision=None):
    return lax.dot_general(
        a, b, ((contract[:1], contract[1:]), ((), ())), precision=precision, preferred_element_type=jnp.float32
    )


def split(x):
    high = x.astype(jnp.bfloat16)
    return high, (x - high.astype(jnp.float32)).astype(jnp.bfloat16)


def precondition(query, factors, scale, modules, side, f_copy):
    chunks = side // GROUP
    width = GROUP * side
    rows = modules * side
    keep = iota((rows, width), 0) % GROUP == iota((rows, width), 1) // side
    fold = zero_one(iota((width, rows), 0) % side == iota((width, rows), 1) % side)
    tile = zero_one(iota((side, width), 0) == iota((side, width), 1) % side)
    gather = zero_one(
        iota((chunks * modules, rows), 0)
        == (iota((chunks * modules, rows), 1) % side) // GROUP * modules + iota((chunks * modules, rows), 1) // side
    )
    block = iota((rows, rows), 0) // side == iota((rows, rows), 1) // side

    spread = [
        jnp.broadcast_to(query[m : m + 1, c * width : (c + 1) * width], (GROUP, width))
        for m in range(modules)
        for c in range(chunks)
    ]
    spread = jnp.where(keep, jnp.concatenate(spread, axis=0), 0.0).astype(jnp.bfloat16)
    matrices = dot(spread, fold, (1, 0)).astype(jnp.bfloat16)

    f_copy.wait()
    lefts = jnp.concatenate([factors[m, 0] for m in range(modules)], axis=0)
    lefts = jnp.where(block, jnp.concatenate([lefts] * modules, axis=1), 0.0)
    left_high, left_low = split(lefts)
    left = dot(left_high, matrices, (1, 0)) + dot(left_low, matrices, (1, 0))
    left = jnp.where(block, left, 0.0)
    high, low = split(left)

    rights = jnp.concatenate([factors[m, 1] for m in range(modules)], axis=0)
    right_high, right_low = split(rights)
    right_high = dot(right_high, tile, (1, 0)).astype(jnp.bfloat16)
    right_low = dot(right_low, tile, (1, 0)).astype(jnp.bfloat16)
    both = dot(high, right_high, (1, 0)) + (dot(low, right_high, (1, 0)) + dot(high, right_low, (1, 0)))
    both = jnp.where(keep, both * (1.0 / scale), 0.0).astype(jnp.bfloat16)
    return dot(gather, both, (1, 0))


def kernel(
    rows_n, grp_scale, q_hbm, t_hbm, f_hbm, out_ref,
    q_v, f_v, t_v, own, held, part, other, pairs, train_v,
    in_sem, t_sem, send_sem, recv_sem, ex_sem,
):
    modules, coords = q_hbm.shape[1:]
    side = f_hbm.shape[-1]
    tiles = coords // LANES
    train = t_hbm.shape[0]
    me = lax.axis_index("rows")
    core = lax.axis_index("mod")

    q_copy = pltpu.make_async_copy(q_hbm, q_v, in_sem.at[0])
    f_copy = pltpu.make_async_copy(f_hbm, f_v, in_sem.at[1])
    q_copy.start()
    f_copy.start()

    barrier = pltpu.get_barrier_semaphore()
    for step in range(1, rows_n):
        pl.semaphore_signal(barrier, inc=1, device_id={"rows": lax.rem(me + step, rows_n)})
    pl.semaphore_signal(barrier, inc=1, device_id={"mod": 1 - core})

    t_copies = [
        pltpu.make_async_copy(t_hbm.at[:, :, pl.ds(j * LANES, LANES)], t_v.at[j], t_sem.at[j]) for j in range(tiles)
    ]

    q_copy.wait()
    scaled = precondition(q_v[0].astype(jnp.float32), f_v, grp_scale, modules, side, f_copy)
    per = GROUP * side // LANES
    for j in range(tiles):
        c, t = divmod(j, per)
        piece = scaled[c * modules : (c + 1) * modules, t * LANES : (t + 1) * LANES].astype(jnp.bfloat16)
        own[j] = piece

    pl.semaphore_wait(barrier, rows_n)

    def target(step):
        down, up = rows_n - step, step - 1
        down = jnp.where(down > me, down, down - 1)
        up = jnp.where(up < me, up, up + 1)
        return jnp.where(2 * me < rows_n, down, up)

    def push(step):
        return pltpu.make_async_remote_copy(
            src_ref=own,
            dst_ref=held.at[me],
            send_sem=send_sem.at[step],
            recv_sem=recv_sem.at[me],
            device_id={"rows": target(step)},
        )

    def arrival(step):
        source = lax.rem(me + step, rows_n)
        return pltpu.make_async_remote_copy(
            src_ref=own,
            dst_ref=held.at[source],
            send_sem=send_sem.at[step],
            recv_sem=recv_sem.at[source],
            device_id={"rows": source},
        )

    for step in range(1, rows_n):
        push(step).start()
    for copy in t_copies:
        copy.start()
    held[me] = own[...]
    for copy in t_copies:
        copy.wait()
    for j in range(tiles):
        train_v[:, j * LANES : (j + 1) * LANES] = t_v[j].reshape(train * modules, LANES)
    for step in range(1, rows_n):
        arrival(step).wait_recv()

    total = jnp.zeros((rows_n * modules, train * modules), jnp.float32)
    b = jnp.concatenate([held[:, j].reshape(rows_n * modules, LANES) for j in range(tiles)], axis=1)
    total = dot(b, train_v[...], (1, 1))
    for k in range(train * modules // LANES):
        pairs[k] = total[:, k * LANES : (k + 1) * LANES]
    shape = (rows_n, train * modules)
    which = iota(shape, 1) % modules
    kept = jnp.zeros(shape, jnp.float32)
    for m in range(modules):
        some = [pairs[k, pl.ds(m, rows_n, stride=modules), :] for k in range(train * modules // LANES)]
        kept = jnp.where(which == m, jnp.concatenate(some, axis=1), kept)
    pick = zero_one(iota((train * modules, train), 0) // modules == iota((train * modules, train), 1))
    high, low = split(kept)
    summed = dot(jnp.concatenate([high, low], axis=0), pick, (1, 0))
    scores = summed[:rows_n] + summed[rows_n:]
    half = rows_n // 2
    part[0] = scores[:half]
    part[1] = scores[half:]
    swap = pltpu.make_async_remote_copy(
        src_ref=part.at[1 - core],
        dst_ref=other,
        send_sem=ex_sem.at[0],
        recv_sem=ex_sem.at[1],
        device_id={"mod": 1 - core},
    )
    swap.start()
    swap.wait_recv()
    out_ref[...] = part[core] + other[...]
    swap.wait_send()
    for step in range(1, rows_n):
        push(step).wait_send()


def shards(rows_n, cores, queries, train_grads, factors):
    _, modules, coords = queries.shape
    train = train_grads.shape[0]
    side = factors.shape[-1]
    tiles = coords // LANES
    scale = math.sqrt(cores * modules * coords)
    half = rows_n // 2
    return pl.pallas_call(
        functools.partial(kernel, rows_n, scale),
        out_shape=pltpu.VMEM((half, train), jnp.float32),
        in_specs=[pl.BlockSpec(memory_space=pltpu.HBM)] * 3,
        out_specs=pl.BlockSpec(memory_space=pltpu.VMEM),
        scratch_shapes=[
            pltpu.VMEM(queries.shape, jnp.bfloat16),
            pltpu.VMEM(factors.shape, jnp.float32),
            pltpu.VMEM((tiles, train, modules, LANES), jnp.bfloat16),
            pltpu.VMEM((tiles, modules, LANES), jnp.bfloat16),
            pltpu.VMEM((rows_n, tiles, modules, LANES), jnp.bfloat16),
            pltpu.VMEM((2, half, train), jnp.float32),
            pltpu.VMEM((half, train), jnp.float32),
            pltpu.VMEM((train * modules // LANES, rows_n * modules, LANES), jnp.float32),
            pltpu.VMEM((train * modules, coords), jnp.bfloat16),
            pltpu.SemaphoreType.DMA((2,)),
            pltpu.SemaphoreType.DMA((tiles,)),
            pltpu.SemaphoreType.DMA((rows_n,)),
            pltpu.SemaphoreType.DMA((rows_n,)),
            pltpu.SemaphoreType.DMA((2,)),
        ],
        compiler_params=pltpu.CompilerParams(
            collective_id=0, has_side_effects=True, vmem_limit_bytes=60 * 1024 * 1024
        ),
    )(queries, train_grads, factors)


def solution(mesh):
    in_specs = (
        P(("grp", "rows"), "mod", None),
        P(("grp", "rows"), "mod", None),
        P("mod", None, None, None),
    )
    out_specs = P(("grp", "mod"), "rows")
    body = functools.partial(shards, mesh.shape["rows"], mesh.shape["mod"])
    return jax.shard_map(body, mesh=mesh, in_specs=in_specs, out_specs=out_specs, check_vma=False)
```

```python
import functools
import math

import jax
import jax.numpy as jnp
from jax import lax
from jax.experimental import pallas as pl
from jax.experimental.pallas import tpu as pltpu
from jax.sharding import PartitionSpec as P

HIGHEST = lax.Precision.HIGHEST
LANES = 128
GROUP = 8


def iota(shape, dim):
    return lax.broadcasted_iota(jnp.int32, shape, dim)


def zero_one(mask):
    return jnp.where(mask, 1.0, 0.0).astype(jnp.bfloat16)


def dot(a, b, contract, precision=None):
    return lax.dot_general(
        a, b, ((contract[:1], contract[1:]), ((), ())), precision=precision, preferred_element_type=jnp.float32
    )


def split(x):
    high = x.astype(jnp.bfloat16)
    return high, (x - high.astype(jnp.float32)).astype(jnp.bfloat16)


def precondition(query, factors, scale, modules, side, f_copy):
    chunks = side // GROUP
    width = GROUP * side
    rows = modules * side
    keep = iota((rows, width), 0) % GROUP == iota((rows, width), 1) // side
    fold = zero_one(iota((width, rows), 0) % side == iota((width, rows), 1) % side)
    tile = zero_one(iota((side, width), 0) == iota((side, width), 1) % side)
    gather = zero_one(
        iota((chunks * modules, rows), 0)
        == (iota((chunks * modules, rows), 1) % side) // GROUP * modules + iota((chunks * modules, rows), 1) // side
    )
    block = iota((rows, rows), 0) // side == iota((rows, rows), 1) // side

    spread = [
        jnp.broadcast_to(query[m : m + 1, c * width : (c + 1) * width], (GROUP, width))
        for m in range(modules)
        for c in range(chunks)
    ]
    spread = jnp.where(keep, jnp.concatenate(spread, axis=0), 0.0).astype(jnp.bfloat16)
    matrices = dot(spread, fold, (1, 0)).astype(jnp.bfloat16)

    f_copy.wait()
    lefts = jnp.concatenate([factors[m, 0] for m in range(modules)], axis=0)
    lefts = jnp.where(block, jnp.concatenate([lefts] * modules, axis=1), 0.0)
    left_high, left_low = split(lefts)
    left = dot(jnp.concatenate([left_high, left_low], axis=0), matrices, (1, 0))
    left = left[:rows] + left[rows:]
    left = jnp.where(block, left, 0.0)
    high, low = split(left)

    rights = jnp.concatenate([factors[m, 1] for m in range(modules)], axis=0)
    right_high, right_low = split(rights)
    right_high = dot(right_high, tile, (1, 0)).astype(jnp.bfloat16)
    right_low = dot(right_low, tile, (1, 0)).astype(jnp.bfloat16)
    stacked = dot(jnp.concatenate([high, low], axis=0), right_high, (1, 0))
    both = stacked[:rows] + (stacked[rows:] + dot(high, right_low, (1, 0)))
    both = jnp.where(keep, both * (1.0 / scale), 0.0).astype(jnp.bfloat16)
    return dot(gather, both, (1, 0))


def kernel(
    rows_n, grp_scale, q_hbm, t_hbm, f_hbm, out_ref,
    q_v, f_v, t_v, own, held, part, other, pairs, train_v,
    in_sem, t_sem, send_sem, recv_sem, ex_sem,
):
    modules, coords = q_hbm.shape[1:]
    side = f_hbm.shape[-1]
    tiles = coords // LANES
    train = t_hbm.shape[0]
    me = lax.axis_index("rows")
    core = lax.axis_index("mod")

    q_copy = pltpu.make_async_copy(q_hbm, q_v, in_sem.at[0])
    f_copy = pltpu.make_async_copy(f_hbm, f_v, in_sem.at[1])
    q_copy.start()
    f_copy.start()

    barrier = pltpu.get_barrier_semaphore()
    for step in range(1, rows_n):
        pl.semaphore_signal(barrier, inc=1, device_id={"rows": lax.rem(me + step, rows_n)})
    pl.semaphore_signal(barrier, inc=1, device_id={"mod": 1 - core})

    t_copies = [
        pltpu.make_async_copy(t_hbm.at[:, :, pl.ds(j * LANES, LANES)], t_v.at[j], t_sem.at[j]) for j in range(tiles)
    ]

    q_copy.wait()
    scaled = precondition(q_v[0].astype(jnp.float32), f_v, grp_scale, modules, side, f_copy)
    per = GROUP * side // LANES
    for j in range(tiles):
        c, t = divmod(j, per)
        piece = scaled[c * modules : (c + 1) * modules, t * LANES : (t + 1) * LANES].astype(jnp.bfloat16)
        own[j] = piece

    pl.semaphore_wait(barrier, rows_n)

    def target(step):
        down, up = rows_n - step, step - 1
        down = jnp.where(down > me, down, down - 1)
        up = jnp.where(up < me, up, up + 1)
        return jnp.where(2 * me < rows_n, down, up)

    def push(step):
        return pltpu.make_async_remote_copy(
            src_ref=own,
            dst_ref=held.at[me],
            send_sem=send_sem.at[step],
            recv_sem=recv_sem.at[me],
            device_id={"rows": target(step)},
        )

    def arrival(step):
        source = lax.rem(me + step, rows_n)
        return pltpu.make_async_remote_copy(
            src_ref=own,
            dst_ref=held.at[source],
            send_sem=send_sem.at[step],
            recv_sem=recv_sem.at[source],
            device_id={"rows": source},
        )

    for step in range(1, rows_n):
        push(step).start()
    for copy in t_copies:
        copy.start()
    held[me] = own[...]
    for copy in t_copies:
        copy.wait()
    for j in range(tiles):
        train_v[:, j * LANES : (j + 1) * LANES] = t_v[j].reshape(train * modules, LANES)
    for step in range(1, rows_n):
        arrival(step).wait_recv()

    total = jnp.zeros((rows_n * modules, train * modules), jnp.float32)
    b = jnp.concatenate([held[:, j].reshape(rows_n * modules, LANES) for j in range(tiles)], axis=1)
    total = dot(b, train_v[...], (1, 1))
    for k in range(train * modules // LANES):
        pairs[k] = total[:, k * LANES : (k + 1) * LANES]
    shape = (rows_n, train * modules)
    which = iota(shape, 1) % modules
    kept = jnp.zeros(shape, jnp.float32)
    for m in range(modules):
        some = [pairs[k, pl.ds(m, rows_n, stride=modules), :] for k in range(train * modules // LANES)]
        kept = jnp.where(which == m, jnp.concatenate(some, axis=1), kept)
    pick = zero_one(iota((train * modules, train), 0) // modules == iota((train * modules, train), 1))
    high, low = split(kept)
    summed = dot(jnp.concatenate([high, low], axis=0), pick, (1, 0))
    scores = summed[:rows_n] + summed[rows_n:]
    half = rows_n // 2
    part[0] = scores[:half]
    part[1] = scores[half:]
    swap = pltpu.make_async_remote_copy(
        src_ref=part.at[1 - core],
        dst_ref=other,
        send_sem=ex_sem.at[0],
        recv_sem=ex_sem.at[1],
        device_id={"mod": 1 - core},
    )
    swap.start()
    swap.wait_recv()
    out_ref[...] = part[core] + other[...]
    swap.wait_send()
    for step in range(1, rows_n):
        push(step).wait_send()


def shards(rows_n, cores, queries, train_grads, factors):
    _, modules, coords = queries.shape
    train = train_grads.shape[0]
    side = factors.shape[-1]
    tiles = coords // LANES
    scale = math.sqrt(cores * modules * coords)
    half = rows_n // 2
    return pl.pallas_call(
        functools.partial(kernel, rows_n, scale),
        out_shape=pltpu.VMEM((half, train), jnp.float32),
        in_specs=[pl.BlockSpec(memory_space=pltpu.HBM)] * 3,
        out_specs=pl.BlockSpec(memory_space=pltpu.VMEM),
        scratch_shapes=[
            pltpu.VMEM(queries.shape, jnp.bfloat16),
            pltpu.VMEM(factors.shape, jnp.float32),
            pltpu.VMEM((tiles, train, modules, LANES), jnp.bfloat16),
            pltpu.VMEM((tiles, modules, LANES), jnp.bfloat16),
            pltpu.VMEM((rows_n, tiles, modules, LANES), jnp.bfloat16),
            pltpu.VMEM((2, half, train), jnp.float32),
            pltpu.VMEM((half, train), jnp.float32),
            pltpu.VMEM((train * modules // LANES, rows_n * modules, LANES), jnp.float32),
            pltpu.VMEM((train * modules, coords), jnp.bfloat16),
            pltpu.SemaphoreType.DMA((2,)),
            pltpu.SemaphoreType.DMA((tiles,)),
            pltpu.SemaphoreType.DMA((rows_n,)),
            pltpu.SemaphoreType.DMA((rows_n,)),
            pltpu.SemaphoreType.DMA((2,)),
        ],
        compiler_params=pltpu.CompilerParams(
            collective_id=0, has_side_effects=True, vmem_limit_bytes=60 * 1024 * 1024
        ),
    )(queries, train_grads, factors)


def solution(mesh):
    in_specs = (
        P(("grp", "rows"), "mod", None),
        P(("grp", "rows"), "mod", None),
        P("mod", None, None, None),
    )
    out_specs = P(("grp", "mod"), "rows")
    body = functools.partial(shards, mesh.shape["rows"], mesh.shape["mod"])
    return jax.shard_map(body, mesh=mesh, in_specs=in_specs, out_specs=out_specs, check_vma=False)
```
